32 devices in a mesh: table: 2 (over x), image: 16 (over z, y, core).
Axes of the slice: x: 2, y: 2, z: 4, core: 2. Of those that a mesh axis runs over, the one named last changes fastest.
Arguments:
- traces: bfloat16 [512, 1920], P(('table', 'image')), may hold values from -6 to 6
- aperture: int32 [512, 4], P(('table', 'image')), may hold values from 0 to 15, all different within a row; in each aligned block of 16 rows (0 to 15, 16 to 31, ...) at most 8 rows name the same one
- bucket: int32 [512], P(('table', 'image')), may hold values from 0 to 3
- table_node: int32 [512, 4], P(('table', 'image')), may hold values from 0 to 15
- entry_gain: bfloat16 [512, 4], P(('table', 'image')), may hold values from 0.5 to 2
- travel: float32 [16, 16, 1024], P('image', None, 'table'), may hold values from 1 to 1918
- spread: float32 [16, 16, 1024], P('image', None, 'table'), may hold values from 0.1 to 1
Outputs:
- image: float32 [16, 1024], P('image', 'table')
The draws below stay inside these ranges and needn't reach their ends.
Inputs may be any that keep to these rules, and one draw needn't show every extreme that they name: `aperture`: each trace names 4 different tiles. Among the 16 traces of one device at most 8 name the same tile, and in every draw some tile is named by exactly 8 of them.
All inputs are finite; a program needn't handle non-finite values.
Results may differ from the reference program's by a relative error of at most 0.0024.
Values may be sent and summed in bfloat16 or wider, within the bound.
A program may use at most 128 MiB of HBM per device.

```python
import math
import jax
import jax.numpy as jnp
import numpy as np
from jax import lax

NS = 1920
TR_DEV = 16
APER = 4
FILTERS = 4
NODES = 16
TILES = 16
CAP = 8
TRACES = 512
CELLS_TILE = 1024
PER_TILE = 128


def touch_ends(drawn, key, smallest, top_value):
    place = [jax.random.randint(jax.random.fold_in(key, axis), (), 0, length) for axis, length in enumerate(drawn.shape)]
    main_axis = drawn.shape.index(max(drawn.shape))
    neighbour = place[:main_axis] + [(place[main_axis] + 1) % drawn.shape[main_axis]] + place[main_axis + 1:]
    return drawn.at[tuple(place)].set(smallest).at[tuple(neighbour)].set(top_value)


def block_levels(rng, dims, split, smallest, top_value):
    level = 1.0
    for dim, shards_of in split:
        steps = jax.random.uniform(jax.random.fold_in(jax.random.fold_in(rng, 6), dim), (shards_of,), jnp.float32, smallest / len(split), top_value / len(split))
        level = level * jnp.repeat(jnp.exp(steps), dims[dim] // shards_of).reshape((-1,) + (1,) * (len(dims) - 1 - dim))
    return level


def deal_out(own_key, own, number, rows, amount, top, reach, slope):
    sequence = jax.random.permutation(own_key, amount)
    packed, usual = portions_of(amount, rows * top, reach, slope, True), portions_of(amount, rows * top, reach, slope, False)
    places = jnp.arange(amount)

    def named(sizes, rotation):
        used = int((sizes > 0).sum())
        fixed = max(1, used // 4)
        passed = fixed + (places - fixed + rotation * (used - fixed)) % max(1, amount - fixed)
        return jnp.zeros((amount,), jnp.int32).at[sequence[jnp.where(places < fixed, places, passed)]].set(jnp.asarray(sizes, jnp.int32))

    sizes = jnp.where(number % 4 == 0, named(packed, number // 4), named(usual, number - number // 4 - 1))
    mixed = jax.random.permutation(jax.random.fold_in(own, 3), amount)
    source_of, sink = mixed[0:amount // 2 * 2:2], mixed[1:amount // 2 * 2:2]
    room = jnp.minimum(sizes[source_of] - 1, reach - sizes[sink]) // 2
    room = jnp.where((source_of == sequence[0]) | (sink == sequence[0]) | (sizes[sink] == 0), 0, jnp.maximum(room, 0))
    passed = jax.random.randint(jax.random.fold_in(own, 4), (amount // 2,), 0, 1 << 20) % (room + 1)
    sizes = sizes.at[source_of].add(-passed).at[sink].add(passed)
    items = jnp.searchsorted(jnp.cumsum(sizes), jnp.arange(rows * top), side="right").astype(jnp.int32)
    listing = items.reshape(top, rows).T
    listing = listing[jax.random.permutation(jax.random.fold_in(own, 1), rows)]
    rotation = jax.random.randint(jax.random.fold_in(own, 2), (rows, 1), 0, top)
    return jnp.take_along_axis(listing, (jnp.arange(top)[None, :] + rotation) % top, axis=1)


def portions_of(amount, total, most, lean, full):
    loads = [(1 << 20) // math.isqrt(rank ** lean) + 1 for rank in range(1, amount + 1)]
    largest = most if full else min(most, max(-(-total // amount), total * loads[0] // sum(loads)))
    least = 1 if total - largest >= amount - 1 else 0
    holding, rest = [largest] + [least] * (amount - 1), total - largest - least * (amount - 1)
    while rest > 0:
        candidates = [i for i in range(1, amount) if holding[i] < largest] or [i for i in range(1, amount) if holding[i] < most]
        pool, left = sum([loads[i] for i in candidates]), rest
        for i in candidates:
            extra = min(most - holding[i], max(1, left * loads[i] // pool), rest)
            holding[i] = holding[i] + extra
            rest = rest - extra
    return np.array(holding)


def scatter_about(rng, dims, scale, limit, cuts=(), dtype=jnp.bfloat16):
    array = jax.random.normal(rng, dims, jnp.float32) * scale
    if len(cuts) > 0:
        array = block_levels(rng, dims, cuts, -0.22, 0.18) * array
    return jnp.clip(array, min=-limit, max=limit).astype(dtype)


def setup_inputs(seed: int = 0) -> dict:
    key_of = jax.random.split(jax.random.key(seed), 8)
    traces = scatter_about(key_of[0], (TRACES, NS), 1.0, 6.0, ((0, 32),))
    aperture_keys = jax.random.split(jax.random.fold_in(key_of[1], 1), TRACES // TR_DEV)
    aperture_turns = jax.random.permutation(jax.random.fold_in(key_of[1], 3), TRACES // TR_DEV)
    aperture = jax.vmap(lambda own, number: deal_out(jax.random.fold_in(key_of[1], 2), own, number, TR_DEV, TILES, APER, CAP, 2))(aperture_keys, aperture_turns).reshape((TRACES, APER))
    bucket = touch_ends(jax.random.randint(key_of[2], (TRACES,), 0, FILTERS), jax.random.fold_in(key_of[2], 1), 0, FILTERS - 1).astype(jnp.int32)
    table_node = touch_ends(jax.random.randint(key_of[3], (TRACES, APER), 0, NODES), jax.random.fold_in(key_of[3], 1), 0, NODES - 1).astype(jnp.int32)
    entry_gain = jnp.clip(jnp.exp(math.log(2.0) - 1.3862944 * jax.random.uniform(key_of[4], (TRACES, APER), jnp.float32) ** block_levels(key_of[4], (TRACES, APER), ((0, 32),), -0.2, 0.2)), 0.5, 2.0).astype(jnp.bfloat16)
    travel = jnp.clip(1.0 + 1917.0 * jax.random.uniform(key_of[5], (TILES, NODES, CELLS_TILE), jnp.float32) ** block_levels(key_of[5], (TILES, NODES, CELLS_TILE), ((0, 16), (2, 2)), -0.2, 0.2), 1.0, 1918.0)
    spread = jnp.clip(jnp.exp(math.log(1.0) - 2.3025851 * jax.random.uniform(key_of[6], (TILES, NODES, CELLS_TILE), jnp.float32) ** block_levels(key_of[6], (TILES, NODES, CELLS_TILE), ((0, 16), (2, 2)), -0.2, 0.2)), 0.1, 1.0)
    return {"traces": traces, "aperture": aperture, "bucket": bucket, "table_node": table_node, "entry_gain": entry_gain, "travel": travel, "spread": spread}


max_lag = 7

def antialias(trace_rows, filter_index):
    half_width = (2 + 2 * filter_index).astype(jnp.float32)[..., None]
    length = trace_rows.shape[-1]
    widths = [(0, 0)] * (trace_rows.ndim - 1) + [(max_lag, max_lag)]
    padded = jnp.pad(trace_rows, widths)
    summed = jnp.zeros(trace_rows.shape, jnp.float32)
    for sample_lag in range(-max_lag, max_lag + 1):
        ramp_weight = jnp.maximum(half_width - abs(sample_lag), 0.0) / (half_width * half_width)
        window = lax.slice_in_dim(padded, max_lag + sample_lag, max_lag + sample_lag + length, axis=trace_rows.ndim - 1)
        summed = summed + ramp_weight * window
    return summed

def interpolate(stack_tile, travel_tile, spread_tile):
    floor_value = jnp.floor(travel_tile)
    fraction = travel_tile - floor_value
    lower_index = floor_value.astype(jnp.int32)
    lower_value = jnp.take_along_axis(stack_tile, lower_index, axis=1)
    upper_value = jnp.take_along_axis(stack_tile, lower_index + 1, axis=1)
    return lax.optimization_barrier(jnp.sum(spread_tile * ((1.0 - fraction) * lower_value + fraction * upper_value), axis=0))

def reference(traces, aperture, bucket, table_node, entry_gain, travel, spread):
    blocks = traces.shape[0] // TR_DEV
    block_traces = traces.reshape(blocks, TR_DEV, NS)
    block_tiles = aperture.reshape(blocks, TR_DEV * APER)
    block_filters = bucket.reshape(blocks, TR_DEV)
    block_nodes = table_node.reshape(blocks, TR_DEV * APER)
    block_gains = entry_gain.reshape(blocks, TR_DEV, APER)

    def accumulate(stack, block):
        trace_rows, row_tiles, row_filters, row_nodes, row_gains = block
        filtered = antialias(trace_rows.astype(jnp.float32), row_filters)
        contribution = (row_gains.astype(jnp.float32)[:, :, None] * filtered[:, None, :]).astype(jnp.bfloat16)
        flat_values = contribution.reshape(TR_DEV * APER, NS).astype(jnp.float32)
        stack = stack.at[row_tiles, row_nodes].add(flat_values)
        return (stack, None)
    initial = jnp.zeros((TILES, NODES, NS), jnp.float32)
    stack, unused = lax.scan(accumulate, initial, (block_traces, block_tiles, block_filters, block_nodes, block_gains))
    image = jax.vmap(interpolate)(stack, travel, spread)
    return image * (1.0 / math.sqrt(PER_TILE))
```

```python
import functools
import math

import jax
import jax.numpy as jnp
from jax import lax
from jax.experimental import pallas as pl
from jax.experimental.pallas import tpu as pltpu
from jax.sharding import PartitionSpec as P

LANES = 128
FILTERS = 4
MESH = pl.DeviceIdType.MESH


def split_axis(count):
    if count == 16:
        return (4, 2, 2)
    root = math.isqrt(count)
    if root * root == count:
        return (root, root, 1)
    return (count, 1, 1)


def peers(size, at):
    found = []
    for step in range(1, size):
        if size & (size - 1):
            found.append(lax.rem(at + step, size))
            continue
        to, bit = at, 1
        while bit <= step:
            if step & bit:
                to = to + bit * (1 - 2 * lax.rem(to // bit, 2))
            bit *= 2
        found.append(to)
    return found


def eye_column(row, count):
    across = lax.broadcasted_iota(jnp.int32, (count, count), 1)
    down = lax.broadcasted_iota(jnp.int32, (count, count), 0)
    return jnp.sum(jnp.where(across == down, row, 0.0), axis=1, keepdims=True)


def selection(aperture, bucket, node, gain, nodes, half):
    count = aperture.shape[1]
    lane = lax.broadcasted_iota(jnp.int32, (count, 2 * half), 1)
    low = lane < half
    tile = jnp.where(low, lane, lane - half).astype(jnp.float32)
    offset = eye_column(bucket.astype(jnp.float32) * nodes, count)
    total = jnp.zeros((count, 2 * half), jnp.float32)
    for a in range(aperture.shape[0]):
        named = eye_column(aperture[a : a + 1].astype(jnp.float32), count)
        row = eye_column(node[a : a + 1].astype(jnp.float32), count) + offset
        weight = eye_column(gain[a : a + 1].astype(jnp.float32), count)
        total = total + jnp.where(named == tile, jnp.where(low, weight, row), 0.0)
    return total


def stack_of(added, nodes):
    count, samples = added.shape
    width = samples + LANES
    padded = jnp.concatenate([added, jnp.zeros((count, LANES), jnp.float32)], axis=1)
    first, second, third, fourth = (
        padded[b * nodes : (b + 1) * nodes] * (1.0 / (2 + 2 * b) ** 2) for b in range(FILTERS)
    )

    def both(values, lag):
        return pltpu.roll(values, lag, 1) + pltpu.roll(values, width - lag, 1)

    inner = (third + 2.0 * fourth) + both(fourth, 2)
    inner = (second + 2.0 * third) + both(inner, 2)
    inner = (first + 2.0 * second + third) + both(inner, 2)
    stack = 2.0 * inner + both(inner, 1)
    upper = pltpu.roll(stack, width - 1, 1)
    return stack[:, :samples], upper[:, :samples]


def partial_image(stack, upper, travel, spread):
    floor_value = jnp.floor(travel)
    fraction = travel - floor_value
    lower = floor_value.astype(jnp.int32)
    chunk = lax.shift_right_logical(lower, 7)
    inner = jnp.bitwise_and(lower, LANES - 1)
    pieces = []
    for c in range(travel.shape[1] // LANES):
        cells = slice(c * LANES, (c + 1) * LANES)
        here, within = chunk[:, cells], inner[:, cells]
        low = jnp.zeros(here.shape, jnp.float32)
        high = jnp.zeros(here.shape, jnp.float32)
        for k in range(stack.shape[1] // LANES):
            samples = slice(k * LANES, (k + 1) * LANES)
            mine = here == k
            picked = jnp.take_along_axis(stack[:, samples], within, axis=1, mode="promise_in_bounds")
            above = jnp.take_along_axis(upper[:, samples], within, axis=1, mode="promise_in_bounds")
            low = jnp.where(mine, picked, low)
            high = jnp.where(mine, above, high)
        part = fraction[:, cells]
        value = spread[:, cells] * ((1.0 - part) * low + part * high)
        pieces.append(jnp.sum(value, axis=0, keepdims=True))
    return jnp.concatenate(pieces, axis=1)


def kernel(
    sizes, groups, half, scale,
    aperture_hbm, bucket_hbm, node_hbm, gain_hbm, traces_ref, travel_ref, spread_ref,
    out_ref,
    aperture_ref, bucket_ref, node_ref, gain_ref,
    blocks, travels, spreads, parts, outgoing,
    load_sem, send_sem, recv_sem, table_send, table_recv, part_send, part_recv,
):
    size_z, size_y, size_c = sizes
    me = lax.axis_index("image")
    group = lax.axis_index("table")
    z = me // (size_y * size_c)
    y = lax.rem(me // size_c, size_y)
    core = lax.rem(me, size_c)
    count, samples = traces_ref.shape
    nodes = travel_ref.shape[0]
    rows = FILTERS * nodes

    def index(at_z, at_y, at_c):
        return (at_z * size_y + at_y) * size_c + at_c

    def slot_of(at_g, at_y, at_c):
        return (at_g * size_y + at_y) * size_c + at_c

    home = slot_of(group, y, core)
    loads = [
        pltpu.make_async_copy(source, landing, load_sem.at[k])
        for k, (source, landing) in enumerate((
            (aperture_hbm, aperture_ref), (bucket_hbm, bucket_ref), (node_hbm, node_ref), (gain_hbm, gain_ref),
            (traces_ref, blocks.at[home, :, pl.ds(0, samples)]),
            (travel_ref, travels.at[z]), (spread_ref, spreads.at[z]),
        ))
    ]
    for load in loads:
        load.start()

    line_z, line_y, line_c = peers(size_z, z), peers(size_y, y), peers(size_c, core)
    line_z = line_z[::-1]
    line_g = peers(groups, group)
    across = [(to_g, to_y) for to_g in line_g for to_y in line_y]
    across += [(to_g, y) for to_g in line_g] + [(group, to_y) for to_y in line_y]

    barrier = pltpu.get_barrier_semaphore()
    partners = [(to_g, index(z, to_y, core)) for to_g, to_y in across]
    partners += [(group, index(z, y, to)) for to in line_c]
    partners += [(group, index(to, y, core)) for to in line_z]
    for partner in partners:
        pl.semaphore_signal(barrier, inc=1, device_id=partner, device_id_type=MESH)

    with jax.named_scope("selection"):
        for load in loads[:4]:
            load.wait()
        blocks[home, :, samples:] = selection(
            aperture_ref[...], bucket_ref[...], node_ref[...], gain_ref[...], nodes, half
        ).astype(jnp.bfloat16)
        lane = lax.broadcasted_iota(jnp.int32, (rows, 2 * half), 1)
        tiles = [index(to, y, core) for to in (*line_z, z)]
        pick_weight = jnp.concatenate([jnp.where(lane == tile, 1.0, 0.0) for tile in tiles], axis=0).astype(jnp.bfloat16)
        pick_row = jnp.concatenate([jnp.where(lane == tile + half, 1.0, 0.0) for tile in tiles], axis=0).astype(jnp.bfloat16)
        loads[4].wait()

    with jax.named_scope("entry_barrier"):
        pl.semaphore_wait(barrier, len(partners))

    started = []

    def block_copy(slot, number, to):
        return pltpu.make_async_remote_copy(
            src_ref=blocks.at[slot],
            dst_ref=blocks.at[slot],
            send_sem=send_sem.at[number],
            recv_sem=recv_sem.at[slot],
            device_id=to,
            device_id_type=MESH,
        )

    def send(slot, to):
        copy = block_copy(slot, len(started), to)
        copy.start()
        started.append(copy)

    def receive(slot):
        block_copy(slot, 0, partners[0]).wait_recv()

    def send_core(slot):
        for to in line_c:
            send(slot, (group, index(z, y, to)))

    for to_g, to_y in across:
        send(home, (to_g, index(z, to_y, core)))
    send_core(home)
    table_copies = []
    for k, to in enumerate(line_z):
        for which, (source, landing) in enumerate(((travel_ref, travels), (spread_ref, spreads))):
            copy = pltpu.make_async_remote_copy(
                src_ref=source,
                dst_ref=landing.at[z],
                send_sem=table_send.at[which, k],
                recv_sem=table_recv.at[which, z],
                device_id=(group, index(to, y, core)),
                device_id_type=MESH,
            )
            copy.start()
            table_copies.append(copy)

    for at_g, at_y in across[::-1]:
        slot = slot_of(at_g, at_y, core)
        receive(slot)
        send_core(slot)
    for at_c in line_c:
        receive(slot_of(group, y, at_c))
    for at_g, at_y in across[::-1]:
        for at_c in line_c:
            receive(slot_of(at_g, at_y, at_c))

    total = groups * size_y * size_c * count
    with jax.named_scope("stack"):
        chosen = blocks[:, :, samples:].reshape(total, 2 * half)
        dims = (((1,), (1,)), ((), ()))
        weight = lax.dot_general(pick_weight, chosen, dims, preferred_element_type=jnp.float32)
        row = lax.dot_general(pick_row, chosen, dims, preferred_element_type=jnp.float32)
        wanted = lax.broadcasted_iota(jnp.int32, (rows, total), 0).astype(jnp.float32)
        data = blocks[:, :, :samples].reshape(total, samples)
        stacks = []
        for k in range(size_z):
            mine = slice(k * rows, (k + 1) * rows)
            member = jnp.where(row[mine] == wanted, weight[mine], 0.0).astype(jnp.bfloat16)
            stacks.append(jnp.dot(member, data, preferred_element_type=jnp.float32))

    part_copies = []
    with jax.named_scope("other_images"):
        for k, to in enumerate(line_z):
            stack, upper = stack_of(stacks[k], nodes)
            for which, landing in enumerate((travels, spreads)):
                pltpu.make_async_remote_copy(
                    src_ref=landing.at[to],
                    dst_ref=landing.at[to],
                    send_sem=table_send.at[which, k],
                    recv_sem=table_recv.at[which, to],
                    device_id=(group, index(to, y, core)),
                    device_id_type=MESH,
                ).wait_recv()
            outgoing[k] = partial_image(stack, upper, travels[to], spreads[to])
            copy = pltpu.make_async_remote_copy(
                src_ref=outgoing.at[k],
                dst_ref=parts.at[z],
                send_sem=part_send.at[k],
                recv_sem=part_recv.at[z],
                device_id=(group, index(to, y, core)),
                device_id_type=MESH,
            )
            copy.start()
            part_copies.append(copy)
    with jax.named_scope("own_image"):
        for load in loads[5:]:
            load.wait()
        stack, upper = stack_of(stacks[size_z - 1], nodes)
        image = partial_image(stack, upper, travels[z], spreads[z])
    with jax.named_scope("last_waits"):
        for copy in started:
            copy.wait_send()
        for copy in table_copies:
            copy.wait_send()
        for k, to in enumerate(line_z):
            pltpu.make_async_remote_copy(
                src_ref=outgoing.at[k],
                dst_ref=parts.at[to],
                send_sem=part_send.at[k],
                recv_sem=part_recv.at[to],
                device_id=(group, index(to, y, core)),
                device_id_type=MESH,
            ).wait_recv()
            image = image + parts[to]
        for copy in part_copies:
            copy.wait_send()
    out_ref[...] = image * scale


def per_device(traces, aperture, bucket, table_node, entry_gain, travel, spread):
    tiles = lax.axis_size("image")
    groups = lax.axis_size("table")
    count, samples = traces.shape
    nodes, cells = travel.shape[1], travel.shape[2]
    half = -(-tiles // (LANES // 2)) * (LANES // 2)
    sizes = split_axis(tiles)
    size_z, size_y = sizes[:2]
    plane = size_y * sizes[2]
    scale = 1.0 / math.sqrt(count * groups * aperture.shape[1])
    vmem = pl.BlockSpec(memory_space=pltpu.VMEM)
    whole = pl.BlockSpec(memory_space=pl.ANY)
    return pl.pallas_call(
        functools.partial(kernel, sizes, groups, half, scale),
        out_shape=jax.ShapeDtypeStruct((1, cells), jnp.float32),
        in_specs=[whole] * 7,
        out_specs=vmem,
        scratch_shapes=[
            pltpu.VMEM(aperture.shape[::-1], jnp.int32),
            pltpu.VMEM((1, count), jnp.int32),
            pltpu.VMEM(table_node.shape[::-1], jnp.int32),
            pltpu.VMEM(entry_gain.shape[::-1], jnp.bfloat16),
            pltpu.VMEM((groups * plane, count, samples + 2 * half), jnp.bfloat16),
            pltpu.VMEM((size_z, nodes, cells), jnp.float32),
            pltpu.VMEM((size_z, nodes, cells), jnp.float32),
            pltpu.VMEM((size_z, 1, cells), jnp.float32),
            pltpu.VMEM((max(size_z - 1, 1), 1, cells), jnp.float32),
            pltpu.SemaphoreType.DMA((7,)),
            pltpu.SemaphoreType.DMA((groups * plane,)),
            pltpu.SemaphoreType.DMA((groups * plane,)),
            pltpu.SemaphoreType.DMA((2, max(size_z - 1, 1))),
            pltpu.SemaphoreType.DMA((2, size_z)),
            pltpu.SemaphoreType.DMA((max(size_z - 1, 1),)),
            pltpu.SemaphoreType.DMA((size_z,)),
        ],
        compiler_params=pltpu.CompilerParams(
            collective_id=0, has_side_effects=True, vmem_limit_bytes=56 * 1024 * 1024
        ),
        cost_estimate=pl.CostEstimate(flops=10**8, bytes_accessed=10**6, transcendentals=0),
    )(aperture.T, bucket.reshape(1, count), table_node.T, entry_gain.T, traces, travel[0], spread[0])


def solution(mesh):
    in_specs = (
        P(("table", "image"), None),
        P(("table", "image"), None),
        P(("table", "image")),
        P(("table", "image"), None),
        P(("table", "image"), None),
        P("image", None, "table"),
        P("image", None, "table"),
    )
    out_specs = P("image", "table")
    return jax.shard_map(
        per_device, mesh=mesh, in_specs=in_specs, out_specs=out_specs, check_vma=False
    )
```

```python
import functools
import math

import jax
import jax.numpy as jnp
from jax import lax
from jax.experimental import pallas as pl
from jax.experimental.pallas import tpu as pltpu
from jax.sharding import PartitionSpec as P

LANES = 128
FILTERS = 4
MESH = pl.DeviceIdType.MESH


def split_axis(count):
    if count == 16:
        return (4, 2, 2)
    root = math.isqrt(count)
    if root * root == count:
        return (root, root, 1)
    return (count, 1, 1)


def peers(size, at):
    found = []
    for step in range(1, size):
        if size & (size - 1):
            found.append(lax.rem(at + step, size))
            continue
        to, bit = at, 1
        while bit <= step:
            if step & bit:
                to = to + bit * (1 - 2 * lax.rem(to // bit, 2))
            bit *= 2
        found.append(to)
    return found


def eye_column(row, count):
    across = lax.broadcasted_iota(jnp.int32, (count, count), 1)
    down = lax.broadcasted_iota(jnp.int32, (count, count), 0)
    return jnp.sum(jnp.where(across == down, row, 0.0), axis=1, keepdims=True)


def selection(aperture, bucket, node, gain, nodes, half):
    count = aperture.shape[1]
    lane = lax.broadcasted_iota(jnp.int32, (count, 2 * half), 1)
    low = lane < half
    tile = jnp.where(low, lane, lane - half).astype(jnp.float32)
    offset = eye_column(bucket.astype(jnp.float32) * nodes, count)
    total = jnp.zeros((count, 2 * half), jnp.float32)
    for a in range(aperture.shape[0]):
        named = eye_column(aperture[a : a + 1].astype(jnp.float32), count)
        row = eye_column(node[a : a + 1].astype(jnp.float32), count) + offset
        weight = eye_column(gain[a : a + 1].astype(jnp.float32), count)
        total = total + jnp.where(named == tile, jnp.where(low, weight, row), 0.0)
    return total


def stack_of(added, nodes):
    count, samples = added.shape
    width = samples + LANES
    padded = jnp.concatenate([added, jnp.zeros((count, LANES), jnp.float32)], axis=1)
    first, second, third, fourth = (
        padded[b * nodes : (b + 1) * nodes] * (1.0 / (2 + 2 * b) ** 2) for b in range(FILTERS)
    )

    def both(values, lag):
        return pltpu.roll(values, lag, 1) + pltpu.roll(values, width - lag, 1)

    inner = (third + 2.0 * fourth) + both(fourth, 2)
    inner = (second + 2.0 * third) + both(inner, 2)
    inner = (first + 2.0 * second + third) + both(inner, 2)
    stack = 2.0 * inner + both(inner, 1)
    upper = pltpu.roll(stack, width - 1, 1)
    return stack[:, :samples], upper[:, :samples]


def partial_image(stack, upper, travel, spread):
    floor_value = jnp.floor(travel)
    fraction = travel - floor_value
    lower = floor_value.astype(jnp.int32)
    chunk = lax.shift_right_logical(lower, 7)
    inner = jnp.bitwise_and(lower, LANES - 1)
    pieces = []
    for c in range(travel.shape[1] // LANES):
        cells = slice(c * LANES, (c + 1) * LANES)
        here, within = chunk[:, cells], inner[:, cells]
        low = jnp.zeros(here.shape, jnp.float32)
        high = jnp.zeros(here.shape, jnp.float32)
        for k in range(stack.shape[1] // LANES):
            samples = slice(k * LANES, (k + 1) * LANES)
            mine = here == k
            picked = jnp.take_along_axis(stack[:, samples], within, axis=1, mode="promise_in_bounds")
            above = jnp.take_along_axis(upper[:, samples], within, axis=1, mode="promise_in_bounds")
            low = jnp.where(mine, picked, low)
            high = jnp.where(mine, above, high)
        part = fraction[:, cells]
        value = spread[:, cells] * ((1.0 - part) * low + part * high)
        pieces.append(jnp.sum(value, axis=0, keepdims=True))
    return jnp.concatenate(pieces, axis=1)


def kernel(
    sizes, groups, half, scale,
    aperture_hbm, bucket_hbm, node_hbm, gain_hbm, traces_ref, travel_ref, spread_ref,
    out_ref,
    aperture_ref, bucket_ref, node_ref, gain_ref,
    blocks, travels, spreads, parts, outgoing,
    load_sem, send_sem, recv_sem, table_send, table_recv, part_send, part_recv,
):
    size_z, size_y, size_c = sizes
    me = lax.axis_index("image")
    group = lax.axis_index("table")
    z = me // (size_y * size_c)
    y = lax.rem(me // size_c, size_y)
    core = lax.rem(me, size_c)
    count, samples = traces_ref.shape
    nodes = travel_ref.shape[0]
    rows = FILTERS * nodes

    def index(at_z, at_y, at_c):
        return (at_z * size_y + at_y) * size_c + at_c

    def slot_of(at_g, at_y, at_c):
        return (at_g * size_y + at_y) * size_c + at_c

    home = slot_of(group, y, core)
    loads = [
        pltpu.make_async_copy(source, landing, load_sem.at[k])
        for k, (source, landing) in enumerate((
            (aperture_hbm, aperture_ref), (bucket_hbm, bucket_ref), (node_hbm, node_ref), (gain_hbm, gain_ref),
            (traces_ref, blocks.at[home, :, pl.ds(0, samples)]),
            (travel_ref, travels.at[z]), (spread_ref, spreads.at[z]),
        ))
    ]
    for load in loads:
        load.start()

    line_z, line_y, line_c = peers(size_z, z), peers(size_y, y), peers(size_c, core)
    line_z = line_z[::-1]
    line_g = peers(groups, group)
    across = [(to_g, to_y) for to_g in line_g for to_y in line_y]
    across += [(to_g, y) for to_g in line_g] + [(group, to_y) for to_y in line_y]

    barrier = pltpu.get_barrier_semaphore()
    partners = [(to_g, index(z, to_y, core)) for to_g, to_y in across]
    partners += [(group, index(z, y, to)) for to in line_c]
    partners += [(group, index(to, y, core)) for to in line_z]
    for partner in partners:
        pl.semaphore_signal(barrier, inc=1, device_id=partner, device_id_type=MESH)

    with jax.named_scope("selection"):
        for load in loads[:4]:
            load.wait()
        blocks[home, :, samples:] = selection(
            aperture_ref[...], bucket_ref[...], node_ref[...], gain_ref[...], nodes, half
        ).astype(jnp.bfloat16)
        lane = lax.broadcasted_iota(jnp.int32, (rows, 2 * half), 1)
        tiles = [index(to, y, core) for to in (*line_z, z)]
        pick_weight = jnp.concatenate([jnp.where(lane == tile, 1.0, 0.0) for tile in tiles], axis=0).astype(jnp.bfloat16)
        pick_row = jnp.concatenate([jnp.where(lane == tile + half, 1.0, 0.0) for tile in tiles], axis=0).astype(jnp.bfloat16)
        loads[4].wait()

    with jax.named_scope("entry_barrier"):
        pl.semaphore_wait(barrier, len(partners))

    started = []

    def block_copy(slot, number, to):
        return pltpu.make_async_remote_copy(
            src_ref=blocks.at[slot],
            dst_ref=blocks.at[slot],
            send_sem=send_sem.at[number],
            recv_sem=recv_sem.at[slot],
            device_id=to,
            device_id_type=MESH,
        )

    def send(slot, to):
        copy = block_copy(slot, len(started), to)
        copy.start()
        started.append(copy)

    def receive(slot):
        block_copy(slot, 0, partners[0]).wait_recv()

    def send_core(slot):
        for to in line_c:
            send(slot, (group, index(z, y, to)))

    for to_g, to_y in across:
        send(home, (to_g, index(z, to_y, core)))
    send_core(home)
    table_copies = []
    for k, to in enumerate(line_z):
        for which, (source, landing) in enumerate(((travel_ref, travels), (spread_ref, spreads))):
            copy = pltpu.make_async_remote_copy(
                src_ref=source,
                dst_ref=landing.at[z],
                send_sem=table_send.at[which, k],
                recv_sem=table_recv.at[which, z],
                device_id=(group, index(to, y, core)),
                device_id_type=MESH,
            )
            copy.start()
            table_copies.append(copy)

    for at_g, at_y in across[::-1]:
        slot = slot_of(at_g, at_y, core)
        receive(slot)
        send_core(slot)
    for at_c in line_c:
        receive(slot_of(group, y, at_c))
    for at_g, at_y in across[::-1]:
        for at_c in line_c:
            receive(slot_of(at_g, at_y, at_c))

    total = groups * size_y * size_c * count
    with jax.named_scope("stack"):
        chosen = blocks[:, :, samples:].reshape(total, 2 * half)
        dims = (((1,), (1,)), ((), ()))
        weight = lax.dot_general(pick_weight, chosen, dims, preferred_element_type=jnp.float32)
        row = lax.dot_general(pick_row, chosen, dims, preferred_element_type=jnp.float32)
        wanted = lax.broadcasted_iota(jnp.int32, (rows, total), 0).astype(jnp.float32)
        data = blocks[:, :, :samples].reshape(total, samples)
        stacks = []
        for k in range(size_z):
            mine = slice(k * rows, (k + 1) * rows)
            member = jnp.where(row[mine] == wanted, weight[mine], 0.0).astype(jnp.bfloat16)
            stacks.append(jnp.dot(member, data, preferred_element_type=jnp.float32))

    part_copies = []
    with jax.named_scope("other_images"):
        for k, to in enumerate(line_z):
            stack, upper = stack_of(stacks[k], nodes)
            for which, landing in enumerate((travels, spreads)):
                pltpu.make_async_remote_copy(
                    src_ref=landing.at[to],
                    dst_ref=landing.at[to],
                    send_sem=table_send.at[which, k],
                    recv_sem=table_recv.at[which, to],
                    device_id=(group, index(to, y, core)),
                    device_id_type=MESH,
                ).wait_recv()
            outgoing[k] = partial_image(stack, upper, travels[to], spreads[to])
            copy = pltpu.make_async_remote_copy(
                src_ref=outgoing.at[k],
                dst_ref=parts.at[z],
                send_sem=part_send.at[k],
                recv_sem=part_recv.at[z],
                device_id=(group, index(to, y, core)),
                device_id_type=MESH,
            )
            copy.start()
            part_copies.append(copy)
    with jax.named_scope("own_image"):
        for load in loads[5:]:
            load.wait()
        stack, upper = stack_of(stacks[size_z - 1], nodes)
        image = partial_image(stack, upper, travels[z], spreads[z])
    with jax.named_scope("last_waits"):
        for copy in started:
            copy.wait_send()
        for copy in table_copies:
            copy.wait_send()
        for k, to in enumerate(line_z):
            pltpu.make_async_remote_copy(
                src_ref=outgoing.at[k],
                dst_ref=parts.at[to],
                send_sem=part_send.at[k],
                recv_sem=part_recv.at[to],
                device_id=(group, index(to, y, core)),
                device_id_type=MESH,
            ).wait_recv()
            image = image + parts[to]
        for copy in part_copies:
            copy.wait_send()
    out_ref[...] = image * scale


def per_device(traces, aperture, bucket, table_node, entry_gain, travel, spread):
    tiles = lax.axis_size("image")
    groups = lax.axis_size("table")
    count, samples = traces.shape
    nodes, cells = travel.shape[1], travel.shape[2]
    half = -(-tiles // (LANES // 2)) * (LANES // 2)
    sizes = split_axis(tiles)
    size_z, size_y = sizes[:2]
    plane = size_y * sizes[2]
    scale = 1.0 / math.sqrt(count * groups * aperture.shape[1])
    vmem = pl.BlockSpec(memory_space=pltpu.VMEM)
    whole = pl.BlockSpec(memory_space=pl.ANY)
    return pl.pallas_call(
        functools.partial(kernel, sizes, groups, half, scale),
        out_shape=jax.ShapeDtypeStruct((1, cells), jnp.float32),
        in_specs=[whole] * 7,
        out_specs=vmem,
        scratch_shapes=[
            pltpu.VMEM(aperture.shape[::-1], jnp.int32),
            pltpu.VMEM((1, count), jnp.int32),
            pltpu.VMEM(table_node.shape[::-1], jnp.int32),
            pltpu.VMEM(entry_gain.shape[::-1], jnp.bfloat16),
            pltpu.VMEM((groups * plane, count, samples + 2 * half), jnp.bfloat16),
            pltpu.VMEM((size_z, nodes, cells), jnp.float32),
            pltpu.VMEM((size_z, nodes, cells), jnp.float32),
            pltpu.VMEM((size_z, 1, cells), jnp.float32),
            pltpu.VMEM((max(size_z - 1, 1), 1, cells), jnp.float32),
            pltpu.SemaphoreType.DMA((7,)),
            pltpu.SemaphoreType.DMA((groups * plane,)),
            pltpu.SemaphoreType.DMA((groups * plane,)),
            pltpu.SemaphoreType.DMA((2, max(size_z - 1, 1))),
            pltpu.SemaphoreType.DMA((2, size_z)),
            pltpu.SemaphoreType.DMA((max(size_z - 1, 1),)),
            pltpu.SemaphoreType.DMA((size_z,)),
        ],
        compiler_params=pltpu.CompilerParams(
            collective_id=0, has_side_effects=True, vmem_limit_bytes=24 * 1024 * 1024
        ),
        cost_estimate=pl.CostEstimate(flops=10**8, bytes_accessed=10**6, transcendentals=0),
    )(*(pltpu.with_memory_space_constraint(operand, pltpu.HBM) for operand in (
        aperture.T, bucket.reshape(1, count), table_node.T, entry_gain.T, traces, travel[0], spread[0]
    )))


def solution(mesh):
    in_specs = (
        P(("table", "image"), None),
        P(("table", "image"), None),
        P(("table", "image")),
        P(("table", "image"), None),
        P(("table", "image"), None),
        P("image", None, "table"),
        P("image", None, "table"),
    )
    out_specs = P("image", "table")
    return jax.shard_map(
        per_device, mesh=mesh, in_specs=in_specs, out_specs=out_specs, check_vma=False
    )
```

```python
import functools
import math

import jax
import jax.numpy as jnp
from jax import lax
from jax.experimental import pallas as pl
from jax.experimental.pallas import tpu as pltpu
from jax.sharding import PartitionSpec as P

LANES = 128
FILTERS = 4
MESH = pl.DeviceIdType.MESH


def split_axis(count):
    if count == 16:
        return (4, 2, 2)
    root = math.isqrt(count)
    if root * root == count:
        return (root, root, 1)
    return (count, 1, 1)


def peers(size, at):
    found = []
    for step in range(1, size):
        if size & (size - 1):
            found.append(lax.rem(at + step, size))
            continue
        to, bit = at, 1
        while bit <= step:
            if step & bit:
                to = to + bit * (1 - 2 * lax.rem(to // bit, 2))
            bit *= 2
        found.append(to)
    return found


def eye_column(row, count):
    across = lax.broadcasted_iota(jnp.int32, (count, count), 1)
    down = lax.broadcasted_iota(jnp.int32, (count, count), 0)
    return jnp.sum(jnp.where(across == down, row, 0.0), axis=1, keepdims=True)


def selection(aperture, bucket, node, gain, nodes, half):
    count = aperture.shape[1]
    lane = lax.broadcasted_iota(jnp.int32, (count, 2 * half), 1)
    low = lane < half
    tile = jnp.where(low, lane, lane - half).astype(jnp.float32)
    offset = eye_column(bucket.astype(jnp.float32) * nodes, count)
    total = jnp.zeros((count, 2 * half), jnp.float32)
    for a in range(aperture.shape[0]):
        named = eye_column(aperture[a : a + 1].astype(jnp.float32), count)
        row = eye_column(node[a : a + 1].astype(jnp.float32), count) + offset
        weight = eye_column(gain[a : a + 1].astype(jnp.float32), count)
        total = total + jnp.where(named == tile, jnp.where(low, weight, row), 0.0)
    return total


def stack_of(added, nodes):
    count, samples = added.shape
    width = samples + LANES
    padded = jnp.concatenate([added, jnp.zeros((count, LANES), jnp.float32)], axis=1)
    first, second, third, fourth = (
        padded[b * nodes : (b + 1) * nodes] * (1.0 / (2 + 2 * b) ** 2) for b in range(FILTERS)
    )

    def both(values, lag):
        return pltpu.roll(values, lag, 1) + pltpu.roll(values, width - lag, 1)

    inner = (third + 2.0 * fourth) + both(fourth, 2)
    inner = (second + 2.0 * third) + both(inner, 2)
    inner = (first + 2.0 * second + third) + both(inner, 2)
    stack = 2.0 * inner + both(inner, 1)
    upper = pltpu.roll(stack, width - 1, 1)
    return stack[:, :samples], upper[:, :samples]


def partial_image(stack, upper, travel, spread):
    floor_value = jnp.floor(travel)
    fraction = travel - floor_value
    lower = floor_value.astype(jnp.int32)
    chunk = lax.shift_right_logical(lower, 7)
    inner = jnp.bitwise_and(lower, LANES - 1)
    pieces = []
    for c in range(travel.shape[1] // LANES):
        cells = slice(c * LANES, (c + 1) * LANES)
        here, within = chunk[:, cells], inner[:, cells]
        low = jnp.zeros(here.shape, jnp.float32)
        high = jnp.zeros(here.shape, jnp.float32)
        for k in range(stack.shape[1] // LANES):
            samples = slice(k * LANES, (k + 1) * LANES)
            mine = here == k
            picked = jnp.take_along_axis(stack[:, samples], within, axis=1, mode="promise_in_bounds")
            above = jnp.take_along_axis(upper[:, samples], within, axis=1, mode="promise_in_bounds")
            low = jnp.where(mine, picked, low)
            high = jnp.where(mine, above, high)
        part = fraction[:, cells]
        value = spread[:, cells] * ((1.0 - part) * low + part * high)
        pieces.append(jnp.sum(value, axis=0, keepdims=True))
    return jnp.concatenate(pieces, axis=1)


def kernel(
    sizes, groups, half, scale,
    aperture_hbm, bucket_hbm, node_hbm, gain_hbm, traces_ref, travel_ref, spread_ref,
    out_ref,
    aperture_ref, bucket_ref, node_ref, gain_ref,
    blocks, travels, spreads, parts, outgoing,
    load_sem, send_sem, recv_sem, table_send, table_recv, part_send, part_recv,
):
    size_z, size_y, size_c = sizes
    me = lax.axis_index("image")
    group = lax.axis_index("table")
    z = me // (size_y * size_c)
    y = lax.rem(me // size_c, size_y)
    core = lax.rem(me, size_c)
    count, samples = traces_ref.shape
    nodes = travel_ref.shape[0]
    rows = FILTERS * nodes

    def index(at_z, at_y, at_c):
        return (at_z * size_y + at_y) * size_c + at_c

    def slot_of(at_g, at_y, at_c):
        return (at_g * size_y + at_y) * size_c + at_c

    home = slot_of(group, y, core)
    loads = [
        pltpu.make_async_copy(source, landing, load_sem.at[k])
        for k, (source, landing) in enumerate((
            (aperture_hbm, aperture_ref), (bucket_hbm, bucket_ref), (node_hbm, node_ref), (gain_hbm, gain_ref),
            (traces_ref, blocks.at[home, :, pl.ds(0, samples)]),
            (travel_ref, travels.at[z]), (spread_ref, spreads.at[z]),
        ))
    ]
    for load in loads:
        load.start()

    line_z, line_y, line_c = peers(size_z, z), peers(size_y, y), peers(size_c, core)
    if size_z == 4:
        line_z = [line_z[0], line_z[2], line_z[1]]
    line_g = peers(groups, group)
    across = [(to_g, to_y) for to_g in line_g for to_y in line_y]
    across += [(to_g, y) for to_g in line_g] + [(group, to_y) for to_y in line_y]

    barrier = pltpu.get_barrier_semaphore()
    partners = [(to_g, index(z, to_y, core)) for to_g, to_y in across]
    partners += [(group, index(z, y, to)) for to in line_c]
    partners += [(group, index(to, y, core)) for to in line_z]
    for partner in partners:
        pl.semaphore_signal(barrier, inc=1, device_id=partner, device_id_type=MESH)

    with jax.named_scope("selection"):
        for load in loads[:4]:
            load.wait()
        blocks[home, :, samples:] = selection(
            aperture_ref[...], bucket_ref[...], node_ref[...], gain_ref[...], nodes, half
        ).astype(jnp.bfloat16)
        lane = lax.broadcasted_iota(jnp.int32, (rows, 2 * half), 1)
        tiles = [index(to, y, core) for to in (*line_z, z)]
        pick_weight = jnp.concatenate([jnp.where(lane == tile, 1.0, 0.0) for tile in tiles], axis=0).astype(jnp.bfloat16)
        pick_row = jnp.concatenate([jnp.where(lane == tile + half, 1.0, 0.0) for tile in tiles], axis=0).astype(jnp.bfloat16)
        loads[4].wait()

    with jax.named_scope("entry_barrier"):
        pl.semaphore_wait(barrier, len(partners))

    started = []

    def block_copy(slot, number, to):
        return pltpu.make_async_remote_copy(
            src_ref=blocks.at[slot],
            dst_ref=blocks.at[slot],
            send_sem=send_sem.at[number],
            recv_sem=recv_sem.at[slot],
            device_id=to,
            device_id_type=MESH,
        )

    def send(slot, to):
        copy = block_copy(slot, len(started), to)
        copy.start()
        started.append(copy)

    def receive(slot):
        block_copy(slot, 0, partners[0]).wait_recv()

    def send_core(slot):
        for to in line_c:
            send(slot, (group, index(z, y, to)))

    for to_g, to_y in across:
        send(home, (to_g, index(z, to_y, core)))
    send_core(home)
    table_copies = []
    for k, to in enumerate(line_z):
        for which, (source, landing) in enumerate(((travel_ref, travels), (spread_ref, spreads))):
            copy = pltpu.make_async_remote_copy(
                src_ref=source,
                dst_ref=landing.at[z],
                send_sem=table_send.at[which, k],
                recv_sem=table_recv.at[which, z],
                device_id=(group, index(to, y, core)),
                device_id_type=MESH,
            )
            copy.start()
            table_copies.append(copy)

    for at_g, at_y in across[::-1]:
        slot = slot_of(at_g, at_y, core)
        receive(slot)
        send_core(slot)
    for at_c in line_c:
        receive(slot_of(group, y, at_c))
    for at_g, at_y in across[::-1]:
        for at_c in line_c:
            receive(slot_of(at_g, at_y, at_c))

    total = groups * size_y * size_c * count
    with jax.named_scope("stack"):
        chosen = blocks[:, :, samples:].reshape(total, 2 * half)
        dims = (((1,), (1,)), ((), ()))
        weight = lax.dot_general(pick_weight, chosen, dims, preferred_element_type=jnp.float32)
        row = lax.dot_general(pick_row, chosen, dims, preferred_element_type=jnp.float32)
        wanted = lax.broadcasted_iota(jnp.int32, (rows, total), 0).astype(jnp.float32)
        data = blocks[:, :, :samples].reshape(total, samples)
        stacks = []
        for k in range(size_z):
            mine = slice(k * rows, (k + 1) * rows)
            member = jnp.where(row[mine] == wanted, weight[mine], 0.0).astype(jnp.bfloat16)
            stacks.append(jnp.dot(member, data, preferred_element_type=jnp.float32))

    filtered = [stack_of(stacks[k], nodes) for k in range(size_z - 1)]
    part_copies = []
    with jax.named_scope("other_images"):
        for k, to in enumerate(line_z):
            stack, upper = filtered[k]
            for which, landing in enumerate((travels, spreads)):
                pltpu.make_async_remote_copy(
                    src_ref=landing.at[to],
                    dst_ref=landing.at[to],
                    send_sem=table_send.at[which, k],
                    recv_sem=table_recv.at[which, to],
                    device_id=(group, index(to, y, core)),
                    device_id_type=MESH,
                ).wait_recv()
            outgoing[k] = partial_image(stack, upper, travels[to], spreads[to])
            copy = pltpu.make_async_remote_copy(
                src_ref=outgoing.at[k],
                dst_ref=parts.at[z],
                send_sem=part_send.at[k],
                recv_sem=part_recv.at[z],
                device_id=(group, index(to, y, core)),
                device_id_type=MESH,
            )
            copy.start()
            part_copies.append(copy)
    with jax.named_scope("own_image"):
        for load in loads[5:]:
            load.wait()
        stack, upper = stack_of(stacks[size_z - 1], nodes)
        image = partial_image(stack, upper, travels[z], spreads[z])
    with jax.named_scope("last_waits"):
        for copy in started:
            copy.wait_send()
        for copy in table_copies:
            copy.wait_send()
        for k, to in enumerate(line_z):
            pltpu.make_async_remote_copy(
                src_ref=outgoing.at[k],
                dst_ref=parts.at[to],
                send_sem=part_send.at[k],
                recv_sem=part_recv.at[to],
                device_id=(group, index(to, y, core)),
                device_id_type=MESH,
            ).wait_recv()
            image = image + parts[to]
        for copy in part_copies:
            copy.wait_send()
    out_ref[...] = image * scale


def per_device(traces, aperture, bucket, table_node, entry_gain, travel, spread):
    tiles = lax.axis_size("image")
    groups = lax.axis_size("table")
    count, samples = traces.shape
    nodes, cells = travel.shape[1], travel.shape[2]
    half = -(-tiles // (LANES // 2)) * (LANES // 2)
    sizes = split_axis(tiles)
    size_z, size_y = sizes[:2]
    plane = size_y * sizes[2]
    scale = 1.0 / math.sqrt(count * groups * aperture.shape[1])
    vmem = pl.BlockSpec(memory_space=pltpu.VMEM)
    whole = pl.BlockSpec(memory_space=pl.ANY)
    return pl.pallas_call(
        functools.partial(kernel, sizes, groups, half, scale),
        out_shape=jax.ShapeDtypeStruct((1, cells), jnp.float32),
        in_specs=[whole] * 7,
        out_specs=vmem,
        scratch_shapes=[
            pltpu.VMEM(aperture.shape[::-1], jnp.int32),
            pltpu.VMEM((1, count), jnp.int32),
            pltpu.VMEM(table_node.shape[::-1], jnp.int32),
            pltpu.VMEM(entry_gain.shape[::-1], jnp.bfloat16),
            pltpu.VMEM((groups * plane, count, samples + 2 * half), jnp.bfloat16),
            pltpu.VMEM((size_z, nodes, cells), jnp.float32),
            pltpu.VMEM((size_z, nodes, cells), jnp.float32),
            pltpu.VMEM((size_z, 1, cells), jnp.float32),
            pltpu.VMEM((max(size_z - 1, 1), 1, cells), jnp.float32),
            pltpu.SemaphoreType.DMA((7,)),
            pltpu.SemaphoreType.DMA((groups * plane,)),
            pltpu.SemaphoreType.DMA((groups * plane,)),
            pltpu.SemaphoreType.DMA((2, max(size_z - 1, 1))),
            pltpu.SemaphoreType.DMA((2, size_z)),
            pltpu.SemaphoreType.DMA((max(size_z - 1, 1),)),
            pltpu.SemaphoreType.DMA((size_z,)),
        ],
        compiler_params=pltpu.CompilerParams(
            collective_id=0, has_side_effects=True, vmem_limit_bytes=24 * 1024 * 1024
        ),
        cost_estimate=pl.CostEstimate(flops=10**8, bytes_accessed=10**6, transcendentals=0),
    )(*(pltpu.with_memory_space_constraint(operand, pltpu.HBM) for operand in (
        aperture.T, bucket.reshape(1, count), table_node.T, entry_gain.T, traces, travel[0], spread[0]
    )))


def solution(mesh):
    in_specs = (
        P(("table", "image"), None),
        P(("table", "image"), None),
        P(("table", "image")),
        P(("table", "image"), None),
        P(("table", "image"), None),
        P("image", None, "table"),
        P("image", None, "table"),
    )
    out_specs = P("image", "table")
    return jax.shard_map(
        per_device, mesh=mesh, in_specs=in_specs, out_specs=out_specs, check_vma=False
    )
```

```python
import functools
import math

import jax
import jax.numpy as jnp
from jax import lax
from jax.experimental import pallas as pl
from jax.experimental.pallas import tpu as pltpu
from jax.sharding import PartitionSpec as P

LANES = 128
IMAGES = ((1, 3, 2), (0, 2, 3), (0, 3, 1), (0, 2, 1))
TABLES = ((1, 3, 2), (0, 2, 3), (0, 3, 1), (0, 2, 1))
LEVELS = 32000.0
FACTORS = ((1,), (2, 1), (1, 2, 1), (0, 0, 2, 1))
FILTERS = 4
MESH = pl.DeviceIdType.MESH


def split_axis(count):
    if count == 16:
        return (4, 2, 2)
    root = math.isqrt(count)
    if root * root == count:
        return (root, root, 1)
    return (count, 1, 1)


def peers(size, at):
    found = []
    for step in range(1, size):
        if size & (size - 1):
            found.append(lax.rem(at + step, size))
            continue
        to, bit = at, 1
        while bit <= step:
            if step & bit:
                to = to + bit * (1 - 2 * lax.rem(to // bit, 2))
            bit *= 2
        found.append(to)
    return found


def choose(at, values):
    found = jnp.int32(values[0])
    for k, value in enumerate(values[1:], 1):
        found = jnp.where(at == k, value, found)
    return found


def eye_column(row, count):
    across = lax.broadcasted_iota(jnp.int32, (count, count), 1)
    down = lax.broadcasted_iota(jnp.int32, (count, count), 0)
    return jnp.sum(jnp.where(across == down, row, 0.0), axis=1, keepdims=True)


def selection(aperture, node, gain, unit, half):
    count = aperture.shape[1]
    lane = lax.broadcasted_iota(jnp.int32, (count, 2 * half), 1)
    low = lane < half
    tile = jnp.where(low, lane, lane - half).astype(jnp.float32)
    total = jnp.zeros((count, 2 * half), jnp.float32)
    for a in range(aperture.shape[0]):
        named = eye_column(aperture[a : a + 1].astype(jnp.float32), count)
        row = eye_column(node[a : a + 1].astype(jnp.float32), count)
        weight = eye_column(gain[a : a + 1].astype(jnp.float32), count) * unit
        total = total + jnp.where(named == tile, jnp.where(low, weight, row), 0.0)
    return total


def antialias(traces, bucket):
    count, samples = traces.shape
    width = samples + LANES
    padded = jnp.concatenate([traces, jnp.zeros((count, LANES), jnp.float32)], axis=1)
    factors = []
    for power in range(FILTERS):
        factor = jnp.zeros(bucket.shape, jnp.float32)
        for b, terms in enumerate(FACTORS):
            if power < len(terms) and terms[power]:
                factor = jnp.where(bucket == b, terms[power] / (2 + 2 * b) ** 2, factor)
        factors.append(factor)

    def both(values, lag):
        return pltpu.roll(values, lag, 1) + pltpu.roll(values, width - lag, 1)

    inner = factors[3] * padded
    for power in (2, 1, 0):
        inner = factors[power] * padded + both(inner, 2)
    return (2.0 * inner + both(inner, 1))[:, :samples]


def partial_image(stack, upper, travel, spread):
    floor_value = jnp.floor(travel)
    fraction = travel - floor_value
    lower = floor_value.astype(jnp.int32)
    chunk = lax.shift_right_logical(lower, 7)
    inner = jnp.bitwise_and(lower, LANES - 1)
    pieces = []
    for c in range(travel.shape[1] // LANES):
        cells = slice(c * LANES, (c + 1) * LANES)
        here, within = chunk[:, cells], inner[:, cells]
        low = jnp.zeros(here.shape, jnp.float32)
        high = jnp.zeros(here.shape, jnp.float32)
        for k in range(stack.shape[1] // LANES):
            samples = slice(k * LANES, (k + 1) * LANES)
            mine = here == k
            picked = jnp.take_along_axis(stack[:, samples], within, axis=1, mode="promise_in_bounds")
            above = jnp.take_along_axis(upper[:, samples], within, axis=1, mode="promise_in_bounds")
            low = jnp.where(mine, picked, low)
            high = jnp.where(mine, above, high)
        part = fraction[:, cells]
        value = spread[:, cells] * ((1.0 - part) * low + part * high)
        pieces.append(jnp.sum(value, axis=0, keepdims=True))
    return jnp.concatenate(pieces, axis=1)


def kernel(
    sizes, groups, half, scale,
    aperture_hbm, bucket_hbm, node_hbm, gain_hbm, traces_ref, travel_ref, spread_ref,
    out_ref,
    aperture_ref, bucket_ref, node_ref, gain_ref,
    traces, blocks, picks, halves, travels, spread_own, spreads, parts, outgoing,
    load_sem, send_sem, recv_sem, table_send, table_recv, part_send, part_recv,
):
    size_z, size_y, size_c = sizes
    me = lax.axis_index("image")
    group = lax.axis_index("table")
    z = me // (size_y * size_c)
    y = lax.rem(me // size_c, size_y)
    core = lax.rem(me, size_c)
    count, samples = traces_ref.shape
    nodes = travel_ref.shape[0]
    rows = nodes

    def index(at_z, at_y, at_c):
        return (at_z * size_y + at_y) * size_c + at_c

    def slot_of(at_g, at_y, at_c):
        return (at_g * size_y + at_y) * size_c + at_c

    home = slot_of(group, y, core)
    line_z, line_y, line_c = peers(size_z, z), peers(size_y, y), peers(size_c, core)
    send_z = line_z
    if size_z == 4:
        line_z = [choose(z, [row[k] for row in IMAGES]) for k in range(3)]
        send_z = [choose(z, [row[k] for row in TABLES]) for k in range(3)]
    line_g = peers(groups, group)
    across = [(to_g, to_y) for to_g in line_g for to_y in line_y]
    across += [(to_g, y) for to_g in line_g] + [(group, to_y) for to_y in line_y]

    barrier = pltpu.get_barrier_semaphore()
    partners = [(to_g, index(z, to_y, core)) for to_g, to_y in across]
    partners += [(group, index(z, y, to)) for to in line_c]
    partners += [(group, index(to, y, core)) for to in line_z]
    for partner in partners:
        pl.semaphore_signal(barrier, inc=1, device_id=partner, device_id_type=MESH)

    loads = [
        pltpu.make_async_copy(source, landing, load_sem.at[k])
        for k, (source, landing) in enumerate((
            (aperture_hbm, aperture_ref), (bucket_hbm, bucket_ref), (node_hbm, node_ref), (gain_hbm, gain_ref),
            (traces_ref, traces),
            (travel_ref, travels.at[z]), (spread_ref, spread_own),
        ))
    ]
    for load in loads:
        load.start()

    with jax.named_scope("selection"):
        for load in loads[:5]:
            load.wait()
        bucket = eye_column(bucket_ref[...].astype(jnp.float32), count)
        smooth = antialias(traces[...].astype(jnp.float32), bucket)
        largest = jnp.maximum(jnp.max(jnp.abs(smooth), axis=1, keepdims=True), 1e-30)
        unit = jnp.exp2(jnp.ceil(jnp.log2(largest))).astype(jnp.bfloat16).astype(jnp.float32)
        levels = jnp.round(smooth * (LEVELS / unit))
        blocks[home] = levels.astype(jnp.int32).astype(jnp.int16)
        picks[home] = selection(aperture_ref[...], node_ref[...], gain_ref[...], unit, half).astype(jnp.bfloat16)
        lane = lax.broadcasted_iota(jnp.int32, (rows, 2 * half), 1)
        tiles = [index(to, y, core) for to in (*line_z, z)]
        pick_weight = jnp.concatenate([jnp.where(lane == tile, 1.0, 0.0) for tile in tiles], axis=0).astype(jnp.bfloat16)
        pick_row = jnp.concatenate([jnp.where(lane == tile + half, 1.0, 0.0) for tile in tiles], axis=0).astype(jnp.bfloat16)
        loads[6].wait()
        spreads[z] = (spread_own[...] * LEVELS + 0.5).astype(jnp.int32).astype(jnp.int16)

    with jax.named_scope("entry_barrier"):
        pl.semaphore_wait(barrier, len(partners))

    started = []

    def block_copies(slot, number, to):
        return [
            pltpu.make_async_remote_copy(
                src_ref=landing.at[slot],
                dst_ref=landing.at[slot],
                send_sem=send_sem.at[which, number],
                recv_sem=recv_sem.at[which, slot],
                device_id=to,
                device_id_type=MESH,
            )
            for which, landing in enumerate((picks, blocks))
        ]

    def send(slot, to):
        copies = block_copies(slot, len(started) // 2, to)
        for copy in copies:
            copy.start()
        started.extend(copies)

    def receive(slot):
        for copy in block_copies(slot, 0, partners[0]):
            copy.wait_recv()

    places = groups * size_y * size_c

    def split(slot):
        whole = blocks[slot].astype(jnp.int32).astype(jnp.float32)
        upper = whole.astype(jnp.bfloat16)
        halves[slot] = upper
        halves[places + slot] = (whole - upper.astype(jnp.float32)).astype(jnp.bfloat16)

    def send_core(slot):
        for to in line_c:
            send(slot, (group, index(z, y, to)))

    for to_g, to_y in across:
        send(home, (to_g, index(z, to_y, core)))
    send_core(home)
    table_copies = []
    for k, to in enumerate(send_z):
        for which, (source, landing) in enumerate(((travel_ref, travels), (spreads.at[z], spreads))):
            copy = pltpu.make_async_remote_copy(
                src_ref=source,
                dst_ref=landing.at[z],
                send_sem=table_send.at[which, k],
                recv_sem=table_recv.at[which, z],
                device_id=(group, index(to, y, core)),
                device_id_type=MESH,
            )
            copy.start()
            table_copies.append(copy)

    split(home)
    for at_g, at_y in across[::-1]:
        slot = slot_of(at_g, at_y, core)
        receive(slot)
        send_core(slot)
        split(slot)
    for at_c in line_c:
        receive(slot_of(group, y, at_c))
        split(slot_of(group, y, at_c))
    for at_g, at_y in across[::-1]:
        for at_c in line_c:
            receive(slot_of(at_g, at_y, at_c))
            split(slot_of(at_g, at_y, at_c))

    total = places * count
    with jax.named_scope("stack"):
        chosen = picks[...].reshape(total, 2 * half)
        dims = (((1,), (1,)), ((), ()))
        weight = lax.dot_general(pick_weight, chosen, dims, preferred_element_type=jnp.float32)
        row = lax.dot_general(pick_row, chosen, dims, preferred_element_type=jnp.float32)
        wanted = lax.rem(lax.broadcasted_iota(jnp.int32, row.shape, 0), rows).astype(jnp.float32)
        member = jnp.where(row == wanted, weight, 0.0).astype(jnp.bfloat16)
        member = jnp.concatenate([member, member], axis=1)
        data = halves[...].reshape(2 * total, samples)
        stacks = jnp.dot(member, data, preferred_element_type=jnp.float32)
        uppers = pltpu.roll(stacks, samples - 1, 1)

    part_copies = []
    with jax.named_scope("other_images"):
        for k, to in enumerate(line_z):
            mine = slice(k * rows, (k + 1) * rows)
            for which, landing in enumerate((travels, spreads)):
                pltpu.make_async_remote_copy(
                    src_ref=landing.at[to],
                    dst_ref=landing.at[to],
                    send_sem=table_send.at[which, k],
                    recv_sem=table_recv.at[which, to],
                    device_id=(group, index(to, y, core)),
                    device_id_type=MESH,
                ).wait_recv()
            other = spreads[to].astype(jnp.int32).astype(jnp.float32)
            outgoing[k] = partial_image(stacks[mine], uppers[mine], travels[to], other) * (1.0 / LEVELS)
            copy = pltpu.make_async_remote_copy(
                src_ref=outgoing.at[k],
                dst_ref=parts.at[z],
                send_sem=part_send.at[k],
                recv_sem=part_recv.at[z],
                device_id=(group, index(to, y, core)),
                device_id_type=MESH,
            )
            copy.start()
            part_copies.append(copy)
    with jax.named_scope("own_image"):
        loads[5].wait()
        mine = slice((size_z - 1) * rows, size_z * rows)
        image = partial_image(stacks[mine], uppers[mine], travels[z], spread_own[...])
    with jax.named_scope("last_waits"):
        for copy in started:
            copy.wait_send()
        for copy in table_copies:
            copy.wait_send()
        for k, to in enumerate(line_z):
            pltpu.make_async_remote_copy(
                src_ref=outgoing.at[k],
                dst_ref=parts.at[to],
                send_sem=part_send.at[k],
                recv_sem=part_recv.at[to],
                device_id=(group, index(to, y, core)),
                device_id_type=MESH,
            ).wait_recv()
            image = image + parts[to]
        for copy in part_copies:
            copy.wait_send()
    out_ref[...] = image * (scale / LEVELS)


def per_device(traces, aperture, bucket, table_node, entry_gain, travel, spread):
    tiles = lax.axis_size("image")
    groups = lax.axis_size("table")
    count, samples = traces.shape
    nodes, cells = travel.shape[1], travel.shape[2]
    half = -(-tiles // (LANES // 2)) * (LANES // 2)
    sizes = split_axis(tiles)
    size_z, size_y = sizes[:2]
    plane = size_y * sizes[2]
    scale = 1.0 / math.sqrt(count * groups * aperture.shape[1])
    vmem = pl.BlockSpec(memory_space=pltpu.VMEM)
    whole = pl.BlockSpec(memory_space=pl.ANY)
    return pl.pallas_call(
        functools.partial(kernel, sizes, groups, half, scale),
        out_shape=jax.ShapeDtypeStruct((1, cells), jnp.float32),
        in_specs=[whole] * 7,
        out_specs=vmem,
        scratch_shapes=[
            pltpu.VMEM(aperture.shape[::-1], jnp.int32),
            pltpu.VMEM((1, count), jnp.int32),
            pltpu.VMEM(table_node.shape[::-1], jnp.int32),
            pltpu.VMEM(entry_gain.shape[::-1], jnp.bfloat16),
            pltpu.VMEM(traces.shape, jnp.bfloat16),
            pltpu.VMEM((groups * plane, count, samples), jnp.int16),
            pltpu.VMEM((groups * plane, count, 2 * half), jnp.bfloat16),
            pltpu.VMEM((2 * groups * plane, count, samples), jnp.bfloat16),
            pltpu.VMEM((size_z, nodes, cells), jnp.float32),
            pltpu.VMEM((nodes, cells), jnp.float32),
            pltpu.VMEM((size_z, nodes, cells), jnp.int16),
            pltpu.VMEM((size_z, 1, cells), jnp.float32),
            pltpu.VMEM((max(size_z - 1, 1), 1, cells), jnp.float32),
            pltpu.SemaphoreType.DMA((7,)),
            pltpu.SemaphoreType.DMA((2, groups * plane)),
            pltpu.SemaphoreType.DMA((2, groups * plane)),
            pltpu.SemaphoreType.DMA((2, max(size_z - 1, 1))),
            pltpu.SemaphoreType.DMA((2, size_z)),
            pltpu.SemaphoreType.DMA((max(size_z - 1, 1),)),
            pltpu.SemaphoreType.DMA((size_z,)),
        ],
        compiler_params=pltpu.CompilerParams(
            collective_id=0, has_side_effects=True, vmem_limit_bytes=24 * 1024 * 1024
        ),
        cost_estimate=pl.CostEstimate(flops=10**8, bytes_accessed=10**6, transcendentals=0),
    )(*(pltpu.with_memory_space_constraint(operand, pltpu.HBM) for operand in (
        aperture.T, bucket.reshape(1, count), table_node.T, entry_gain.T, traces, travel[0], spread[0]
    )))


def solution(mesh):
    in_specs = (
        P(("table", "image"), None),
        P(("table", "image"), None),
        P(("table", "image")),
        P(("table", "image"), None),
        P(("table", "image"), None),
        P("image", None, "table"),
        P("image", None, "table"),
    )
    out_specs = P("image", "table")
    return jax.shard_map(
        per_device, mesh=mesh, in_specs=in_specs, out_specs=out_specs, check_vma=False
    )
```

```python
import functools
import math

import jax
import jax.numpy as jnp
from jax import lax
from jax.experimental import pallas as pl
from jax.experimental.pallas import tpu as pltpu
from jax.sharding import PartitionSpec as P

LANES = 128
IMAGES = ((1, 3, 2), (0, 2, 3), (0, 3, 1), (0, 2, 1))
TABLES = ((3, 2, 1), (0, 3, 2), (3, 0, 1), (2, 1, 0))
LEVELS = 32000.0
FACTORS = ((1,), (2, 1), (1, 2, 1), (0, 0, 2, 1))
FILTERS = 4
MESH = pl.DeviceIdType.MESH


def split_axis(count):
    if count == 16:
        return (4, 2, 2)
    root = math.isqrt(count)
    if root * root == count:
        return (root, root, 1)
    return (count, 1, 1)


def peers(size, at):
    found = []
    for step in range(1, size):
        if size & (size - 1):
            found.append(lax.rem(at + step, size))
            continue
        to, bit = at, 1
        while bit <= step:
            if step & bit:
                to = to + bit * (1 - 2 * lax.rem(to // bit, 2))
            bit *= 2
        found.append(to)
    return found


def choose(at, values):
    found = jnp.int32(values[0])
    for k, value in enumerate(values[1:], 1):
        found = jnp.where(at == k, value, found)
    return found


def eye_column(row, count):
    across = lax.broadcasted_iota(jnp.int32, (count, count), 1)
    down = lax.broadcasted_iota(jnp.int32, (count, count), 0)
    return jnp.sum(jnp.where(across == down, row, 0.0), axis=1, keepdims=True)


def selection(aperture, node, gain, half):
    count = aperture.shape[1]
    lane = lax.broadcasted_iota(jnp.int32, (count, 2 * half), 1)
    low = lane < half
    tile = jnp.where(low, lane, lane - half).astype(jnp.float32)
    total = jnp.zeros((count, 2 * half), jnp.float32)
    for a in range(aperture.shape[0]):
        named = eye_column(aperture[a : a + 1].astype(jnp.float32), count)
        row = eye_column(node[a : a + 1].astype(jnp.float32), count)
        weight = eye_column(gain[a : a + 1].astype(jnp.float32), count)
        total = total + jnp.where(named == tile, jnp.where(low, weight, row), 0.0)
    return total


def antialias(traces, bucket):
    count, samples = traces.shape
    width = samples + LANES
    padded = jnp.concatenate([traces, jnp.zeros((count, LANES), jnp.float32)], axis=1)
    factors = []
    for power in range(FILTERS):
        factor = jnp.zeros(bucket.shape, jnp.float32)
        for b, terms in enumerate(FACTORS):
            if power < len(terms) and terms[power]:
                factor = jnp.where(bucket == b, terms[power] / (2 + 2 * b) ** 2, factor)
        factors.append(factor)

    def both(values, lag):
        return pltpu.roll(values, lag, 1) + pltpu.roll(values, width - lag, 1)

    inner = factors[3] * padded
    for power in (2, 1, 0):
        inner = factors[power] * padded + both(inner, 2)
    return (2.0 * inner + both(inner, 1))[:, :samples]


def partial_image(stack, unit, travel, spread):
    floor_value = jnp.floor(travel)
    fraction = travel - floor_value
    lower = floor_value.astype(jnp.int32)
    chunk = lax.shift_right_logical(lower, 7)
    inner = jnp.bitwise_and(lower, LANES - 1)
    pieces = []
    for c in range(travel.shape[1] // LANES):
        cells = slice(c * LANES, (c + 1) * LANES)
        here, within = chunk[:, cells], inner[:, cells]
        pair = jnp.zeros(here.shape, jnp.int32)
        for k in range(stack.shape[1] // LANES):
            samples = slice(k * LANES, (k + 1) * LANES)
            mine = here == k
            picked = jnp.take_along_axis(stack[:, samples], within, axis=1, mode="promise_in_bounds")
            pair = jnp.where(mine, picked, pair)
        high = lax.shift_right_arithmetic(pair, 16)
        low = (pair - lax.shift_left(high, 16)).astype(jnp.float32) - 32768.0
        high = high.astype(jnp.float32)
        part = fraction[:, cells]
        value = spread[:, cells] * ((1.0 - part) * low + part * high)
        pieces.append(jnp.sum(value * unit, axis=0, keepdims=True))
    return jnp.concatenate(pieces, axis=1)


def kernel(
    sizes, groups, half, scale,
    aperture_hbm, bucket_hbm, node_hbm, gain_hbm, traces_ref, travel_ref, spread_ref,
    out_ref,
    aperture_ref, bucket_ref, node_ref, gain_ref,
    traces, blocks, picks, halves, travels, spread_own, spreads, parts, outgoing,
    load_sem, send_sem, recv_sem, table_send, table_recv, part_send, part_recv,
):
    size_z, size_y, size_c = sizes
    me = lax.axis_index("image")
    group = lax.axis_index("table")
    z = me // (size_y * size_c)
    y = lax.rem(me // size_c, size_y)
    core = lax.rem(me, size_c)
    count, samples = traces_ref.shape
    nodes = travel_ref.shape[0]
    rows = nodes

    def index(at_z, at_y, at_c):
        return (at_z * size_y + at_y) * size_c + at_c

    def slot_of(at_g, at_y, at_c):
        return (at_g * size_y + at_y) * size_c + at_c

    home = slot_of(group, y, core)
    line_z, line_y, line_c = peers(size_z, z), peers(size_y, y), peers(size_c, core)
    send_z = line_z
    if size_z == 4:
        line_z = [choose(z, [row[k] for row in IMAGES]) for k in range(3)]
        send_z = [choose(z, [row[k] for row in TABLES]) for k in range(3)]
    line_g = peers(groups, group)
    across = [(to_g, to_y) for to_g in line_g for to_y in line_y]
    across += [(to_g, y) for to_g in line_g] + [(group, to_y) for to_y in line_y]

    loads = [
        pltpu.make_async_copy(source, landing, load_sem.at[k])
        for k, (source, landing) in enumerate((
            (aperture_hbm, aperture_ref), (bucket_hbm, bucket_ref), (node_hbm, node_ref), (gain_hbm, gain_ref),
            (traces_ref, traces),
            (travel_ref, travels.at[z]), (spread_ref, spread_own),
        ))
    ]
    for k in (0, 1, 2, 3, 4, 6, 5):
        loads[k].start()

    barrier = pltpu.get_barrier_semaphore()
    partners = [(to_g, index(z, to_y, core)) for to_g, to_y in across]
    partners += [(group, index(z, y, to)) for to in line_c]
    partners += [(group, index(to, y, core)) for to in line_z]
    for partner in partners:
        pl.semaphore_signal(barrier, inc=1, device_id=partner, device_id_type=MESH)

    with jax.named_scope("selection"):
        for load in loads[:4]:
            load.wait()
        bucket = eye_column(bucket_ref[...].astype(jnp.float32), count)
        chosen = selection(aperture_ref[...], node_ref[...], gain_ref[...], half)
        lane = lax.broadcasted_iota(jnp.int32, chosen.shape, 1)
        loads[4].wait()
        smooth = antialias(traces[...].astype(jnp.float32), bucket)
        largest = jnp.maximum(jnp.max(jnp.abs(smooth), axis=1, keepdims=True), 1e-30)
        unit = jnp.exp2(jnp.ceil(jnp.log2(largest))).astype(jnp.bfloat16).astype(jnp.float32)
        levels = jnp.round(smooth * (LEVELS / unit))
        blocks[home] = levels.astype(jnp.int32).astype(jnp.int16)
        picks[home] = jnp.where(lane < half, chosen * unit, chosen).astype(jnp.bfloat16)

    with jax.named_scope("entry_barrier"):
        pl.semaphore_wait(barrier, len(partners))

    started = []

    def block_copies(slot, number, to):
        return [
            pltpu.make_async_remote_copy(
                src_ref=landing.at[slot],
                dst_ref=landing.at[slot],
                send_sem=send_sem.at[which, number],
                recv_sem=recv_sem.at[which, slot],
                device_id=to,
                device_id_type=MESH,
            )
            for which, landing in enumerate((picks, blocks))
        ]

    def send(slot, to):
        copies = block_copies(slot, len(started) // 2, to)
        for copy in copies:
            copy.start()
        started.extend(copies)

    def receive(slot):
        for copy in block_copies(slot, 0, partners[0]):
            copy.wait_recv()

    places = groups * size_y * size_c

    def split(slot):
        whole = blocks[slot].astype(jnp.int32).astype(jnp.float32)
        upper = whole.astype(jnp.bfloat16)
        halves[slot] = upper
        halves[places + slot] = (whole - upper.astype(jnp.float32)).astype(jnp.bfloat16)

    def send_core(slot):
        for to in line_c:
            send(slot, (group, index(z, y, to)))

    for to_g, to_y in across:
        send(home, (to_g, index(z, to_y, core)))
    send_core(home)
    with jax.named_scope("spread_levels"):
        loads[6].wait()
        spreads[z] = (spread_own[...] * LEVELS + 0.5).astype(jnp.int32).astype(jnp.int16)
    table_copies = []
    for k, to in enumerate(send_z):
        for which, (source, landing) in enumerate(((travel_ref, travels), (spreads.at[z], spreads))):
            copy = pltpu.make_async_remote_copy(
                src_ref=source,
                dst_ref=landing.at[z],
                send_sem=table_send.at[which, k],
                recv_sem=table_recv.at[which, z],
                device_id=(group, index(to, y, core)),
                device_id_type=MESH,
            )
            copy.start()
            table_copies.append(copy)

    with jax.named_scope("picks"):
        lane = lax.broadcasted_iota(jnp.int32, (rows, 2 * half), 1)
        tiles = [index(to, y, core) for to in (*line_z, z)]
        pick_weight = jnp.concatenate([jnp.where(lane == tile, 1.0, 0.0) for tile in tiles], axis=0).astype(jnp.bfloat16)
        pick_row = jnp.concatenate([jnp.where(lane == tile + half, 1.0, 0.0) for tile in tiles], axis=0).astype(jnp.bfloat16)
    split(home)
    for at_g, at_y in across[::-1]:
        slot = slot_of(at_g, at_y, core)
        receive(slot)
        send_core(slot)
        split(slot)
    for at_c in line_c:
        receive(slot_of(group, y, at_c))
        split(slot_of(group, y, at_c))
    for at_g, at_y in across[::-1]:
        for at_c in line_c:
            receive(slot_of(at_g, at_y, at_c))
            split(slot_of(at_g, at_y, at_c))

    total = places * count
    with jax.named_scope("stack"):
        chosen = picks[...].reshape(total, 2 * half)
        dims = (((1,), (1,)), ((), ()))
        weight = lax.dot_general(pick_weight, chosen, dims, preferred_element_type=jnp.float32)
        row = lax.dot_general(pick_row, chosen, dims, preferred_element_type=jnp.float32)
        wanted = lax.rem(lax.broadcasted_iota(jnp.int32, row.shape, 0), rows).astype(jnp.float32)
        member = jnp.where(row == wanted, weight, 0.0).astype(jnp.bfloat16)
        member = jnp.concatenate([member, member], axis=1)
        data = halves[...].reshape(2 * total, samples)
        stacks = jnp.dot(member, data, preferred_element_type=jnp.float32)
        largest = jnp.maximum(jnp.max(jnp.abs(stacks), axis=1, keepdims=True), 1e-30)
        uppers = largest * (1.0 / LEVELS)
        level = jnp.round(stacks * (LEVELS / largest)).astype(jnp.int32)
        stacks = lax.shift_left(pltpu.roll(level, samples - 1, 1), 16) + (level + 32768)

    part_copies = []
    with jax.named_scope("other_images"):
        for k, to in enumerate(line_z):
            mine = slice(k * rows, (k + 1) * rows)
            for which, landing in enumerate((travels, spreads)):
                pltpu.make_async_remote_copy(
                    src_ref=landing.at[to],
                    dst_ref=landing.at[to],
                    send_sem=table_send.at[which, k],
                    recv_sem=table_recv.at[which, to],
                    device_id=(group, index(to, y, core)),
                    device_id_type=MESH,
                ).wait_recv()
            other = spreads[to].astype(jnp.int32).astype(jnp.float32)
            outgoing[k] = partial_image(stacks[mine], uppers[mine], travels[to], other) * (1.0 / LEVELS)
            copy = pltpu.make_async_remote_copy(
                src_ref=outgoing.at[k],
                dst_ref=parts.at[z],
                send_sem=part_send.at[k],
                recv_sem=part_recv.at[z],
                device_id=(group, index(to, y, core)),
                device_id_type=MESH,
            )
            copy.start()
            part_copies.append(copy)
    with jax.named_scope("own_image"):
        loads[5].wait()
        mine = slice((size_z - 1) * rows, size_z * rows)
        image = partial_image(stacks[mine], uppers[mine], travels[z], spread_own[...])
    with jax.named_scope("last_waits"):
        for copy in started:
            copy.wait_send()
        for copy in table_copies:
            copy.wait_send()
        for k, to in enumerate(line_z):
            pltpu.make_async_remote_copy(
                src_ref=outgoing.at[k],
                dst_ref=parts.at[to],
                send_sem=part_send.at[k],
                recv_sem=part_recv.at[to],
                device_id=(group, index(to, y, core)),
                device_id_type=MESH,
            ).wait_recv()
            image = image + parts[to]
        for copy in part_copies:
            copy.wait_send()
    out_ref[...] = image * (scale / LEVELS)


def per_device(traces, aperture, bucket, table_node, entry_gain, travel, spread):
    tiles = lax.axis_size("image")
    groups = lax.axis_size("table")
    count, samples = traces.shape
    nodes, cells = travel.shape[1], travel.shape[2]
    half = -(-tiles // (LANES // 2)) * (LANES // 2)
    sizes = split_axis(tiles)
    size_z, size_y = sizes[:2]
    plane = size_y * sizes[2]
    scale = 1.0 / math.sqrt(count * groups * aperture.shape[1])
    vmem = pl.BlockSpec(memory_space=pltpu.VMEM)
    whole = pl.BlockSpec(memory_space=pl.ANY)
    return pl.pallas_call(
        functools.partial(kernel, sizes, groups, half, scale),
        out_shape=jax.ShapeDtypeStruct((1, cells), jnp.float32),
        in_specs=[whole] * 7,
        out_specs=vmem,
        scratch_shapes=[
            pltpu.VMEM(aperture.shape[::-1], jnp.int32),
            pltpu.VMEM((1, count), jnp.int32),
            pltpu.VMEM(table_node.shape[::-1], jnp.int32),
            pltpu.VMEM(entry_gain.shape[::-1], jnp.bfloat16),
            pltpu.VMEM(traces.shape, jnp.bfloat16),
            pltpu.VMEM((groups * plane, count, samples), jnp.int16),
            pltpu.VMEM((groups * plane, count, 2 * half), jnp.bfloat16),
            pltpu.VMEM((2 * groups * plane, count, samples), jnp.bfloat16),
            pltpu.VMEM((size_z, nodes, cells), jnp.float32),
            pltpu.VMEM((nodes, cells), jnp.float32),
            pltpu.VMEM((size_z, nodes, cells), jnp.int16),
            pltpu.VMEM((size_z, 1, cells), jnp.float32),
            pltpu.VMEM((max(size_z - 1, 1), 1, cells), jnp.float32),
            pltpu.SemaphoreType.DMA((7,)),
            pltpu.SemaphoreType.DMA((2, groups * plane)),
            pltpu.SemaphoreType.DMA((2, groups * plane)),
            pltpu.SemaphoreType.DMA((2, max(size_z - 1, 1))),
            pltpu.SemaphoreType.DMA((2, size_z)),
            pltpu.SemaphoreType.DMA((max(size_z - 1, 1),)),
            pltpu.SemaphoreType.DMA((size_z,)),
        ],
        compiler_params=pltpu.CompilerParams(
            collective_id=0, has_side_effects=True, vmem_limit_bytes=24 * 1024 * 1024
        ),
        cost_estimate=pl.CostEstimate(flops=10**8, bytes_accessed=10**6, transcendentals=0),
    )(*(pltpu.with_memory_space_constraint(operand, pltpu.HBM) for operand in (
        aperture.T, bucket.reshape(1, count), table_node.T, entry_gain.T, traces, travel[0], spread[0]
    )))


def solution(mesh):
    in_specs = (
        P(("table", "image"), None),
        P(("table", "image"), None),
        P(("table", "image")),
        P(("table", "image"), None),
        P(("table", "image"), None),
        P("image", None, "table"),
        P("image", None, "table"),
    )
    out_specs = P("image", "table")
    return jax.shard_map(
        per_device, mesh=mesh, in_specs=in_specs, out_specs=out_specs, check_vma=False
    )
```

```python
import functools
import math

import jax
import jax.numpy as jnp
from jax import lax
from jax.experimental import pallas as pl
from jax.experimental.pallas import tpu as pltpu
from jax.sharding import PartitionSpec as P

LANES = 128
IMAGES = ((1, 3, 2), (0, 2, 3), (0, 3, 1), (0, 2, 1))
TABLES = ((3, 2, 1), (0, 3, 2), (3, 0, 1), (2, 1, 0))
LEVELS = 32000.0
FACTORS = ((1,), (2, 1), (1, 2, 1), (0, 0, 2, 1))
FILTERS = 4
MESH = pl.DeviceIdType.MESH


def split_axis(count):
    if count == 16:
        return (4, 2, 2)
    root = math.isqrt(count)
    if root * root == count:
        return (root, root, 1)
    return (count, 1, 1)


def peers(size, at):
    found = []
    for step in range(1, size):
        if size & (size - 1):
            found.append(lax.rem(at + step, size))
            continue
        to, bit = at, 1
        while bit <= step:
            if step & bit:
                to = to + bit * (1 - 2 * lax.rem(to // bit, 2))
            bit *= 2
        found.append(to)
    return found


def choose(at, values):
    found = jnp.int32(values[0])
    for k, value in enumerate(values[1:], 1):
        found = jnp.where(at == k, value, found)
    return found


def eye_column(row, count):
    across = lax.broadcasted_iota(jnp.int32, (count, count), 1)
    down = lax.broadcasted_iota(jnp.int32, (count, count), 0)
    return jnp.sum(jnp.where(across == down, row, 0.0), axis=1, keepdims=True)


def selection(aperture, node, gain, half):
    count = aperture.shape[1]
    lane = lax.broadcasted_iota(jnp.int32, (count, 2 * half), 1)
    low = lane < half
    tile = jnp.where(low, lane, lane - half).astype(jnp.float32)
    total = jnp.zeros((count, 2 * half), jnp.float32)
    for a in range(aperture.shape[0]):
        named = eye_column(aperture[a : a + 1].astype(jnp.float32), count)
        row = eye_column(node[a : a + 1].astype(jnp.float32), count)
        weight = eye_column(gain[a : a + 1].astype(jnp.float32), count)
        total = total + jnp.where(named == tile, jnp.where(low, weight, row), 0.0)
    return total


def antialias(traces, bucket):
    count, samples = traces.shape
    width = samples + LANES
    padded = jnp.concatenate([traces, jnp.zeros((count, LANES), jnp.float32)], axis=1)
    factors = []
    for power in range(FILTERS):
        factor = jnp.zeros(bucket.shape, jnp.float32)
        for b, terms in enumerate(FACTORS):
            if power < len(terms) and terms[power]:
                factor = jnp.where(bucket == b, terms[power] / (2 + 2 * b) ** 2, factor)
        factors.append(factor)

    def both(values, lag):
        return pltpu.roll(values, lag, 1) + pltpu.roll(values, width - lag, 1)

    inner = factors[3] * padded
    for power in (2, 1, 0):
        inner = factors[power] * padded + both(inner, 2)
    return (2.0 * inner + both(inner, 1))[:, :samples]


def partial_image(stack, upper, travel, spread):
    floor_value = jnp.floor(travel)
    fraction = travel - floor_value
    lower = floor_value.astype(jnp.int32)
    chunk = lax.shift_right_logical(lower, 7)
    inner = jnp.bitwise_and(lower, LANES - 1)
    pieces = []
    for c in range(travel.shape[1] // LANES):
        cells = slice(c * LANES, (c + 1) * LANES)
        here, within = chunk[:, cells], inner[:, cells]
        low = jnp.zeros(here.shape, jnp.float32)
        high = jnp.zeros(here.shape, jnp.float32)
        for k in range(stack.shape[1] // LANES):
            samples = slice(k * LANES, (k + 1) * LANES)
            mine = here == k
            picked = jnp.take_along_axis(stack[:, samples], within, axis=1, mode="promise_in_bounds")
            above = jnp.take_along_axis(upper[:, samples], within, axis=1, mode="promise_in_bounds")
            low = jnp.where(mine, picked, low)
            high = jnp.where(mine, above, high)
        part = fraction[:, cells]
        value = spread[:, cells] * ((1.0 - part) * low + part * high)
        pieces.append(jnp.sum(value, axis=0, keepdims=True))
    return jnp.concatenate(pieces, axis=1)


def kernel(
    sizes, groups, half, scale,
    aperture_hbm, bucket_hbm, node_hbm, gain_hbm, traces_ref, travel_ref, spread_ref,
    out_ref,
    aperture_ref, bucket_ref, node_ref, gain_ref,
    traces, blocks, picks, halves, travels, spread_own, spreads, parts, outgoing,
    load_sem, send_sem, recv_sem, table_send, table_recv, part_send, part_recv,
):
    size_z, size_y, size_c = sizes
    me = lax.axis_index("image")
    group = lax.axis_index("table")
    z = me // (size_y * size_c)
    y = lax.rem(me // size_c, size_y)
    core = lax.rem(me, size_c)
    count, samples = traces_ref.shape
    nodes = travel_ref.shape[0]
    rows = nodes

    def index(at_z, at_y, at_c):
        return (at_z * size_y + at_y) * size_c + at_c

    def slot_of(at_g, at_y, at_c):
        return (at_g * size_y + at_y) * size_c + at_c

    home = slot_of(group, y, core)
    line_z, line_y, line_c = peers(size_z, z), peers(size_y, y), peers(size_c, core)
    send_z = line_z
    if size_z == 4:
        line_z = [choose(z, [row[k] for row in IMAGES]) for k in range(3)]
        send_z = [choose(z, [row[k] for row in TABLES]) for k in range(3)]
    line_g = peers(groups, group)
    across = [(to_g, to_y) for to_g in line_g for to_y in line_y]
    across += [(to_g, y) for to_g in line_g] + [(group, to_y) for to_y in line_y]

    loads = [
        pltpu.make_async_copy(source, landing, load_sem.at[k])
        for k, (source, landing) in enumerate((
            (aperture_hbm, aperture_ref), (bucket_hbm, bucket_ref), (node_hbm, node_ref), (gain_hbm, gain_ref),
            (traces_ref, traces),
            (travel_ref, travels.at[z]), (spread_ref, spread_own),
        ))
    ]
    for k in (4, 1, 0, 2, 3):
        loads[k].start()

    barrier = pltpu.get_barrier_semaphore()
    partners = [(to_g, index(z, to_y, core)) for to_g, to_y in across]
    partners += [(group, index(z, y, to)) for to in line_c]
    partners += [(group, index(to, y, core)) for to in line_z]
    for partner in partners:
        pl.semaphore_signal(barrier, inc=1, device_id=partner, device_id_type=MESH)

    with jax.named_scope("selection"):
        for load in loads[:4]:
            load.wait()
        bucket = eye_column(bucket_ref[...].astype(jnp.float32), count)
        chosen = selection(aperture_ref[...], node_ref[...], gain_ref[...], half)
        lane = lax.broadcasted_iota(jnp.int32, chosen.shape, 1)
        loads[4].wait()
        smooth = antialias(traces[...].astype(jnp.float32), bucket)
        largest = jnp.maximum(jnp.max(jnp.abs(smooth), axis=1, keepdims=True), 1e-30)
        unit = jnp.exp2(jnp.ceil(jnp.log2(largest))).astype(jnp.bfloat16).astype(jnp.float32)
        levels = jnp.round(smooth * (LEVELS / unit))
        blocks[home] = levels.astype(jnp.int32).astype(jnp.int16)
        picks[home] = jnp.where(lane < half, chosen * unit, chosen).astype(jnp.bfloat16)

    for k in (6, 5):
        loads[k].start()
    with jax.named_scope("entry_barrier"):
        pl.semaphore_wait(barrier, len(partners))

    started = []

    def block_copies(slot, number, to):
        return [
            pltpu.make_async_remote_copy(
                src_ref=landing.at[slot],
                dst_ref=landing.at[slot],
                send_sem=send_sem.at[which, number],
                recv_sem=recv_sem.at[which, slot],
                device_id=to,
                device_id_type=MESH,
            )
            for which, landing in enumerate((blocks, picks))
        ]

    def send(slot, to):
        copies = block_copies(slot, len(started) // 2, to)
        for copy in copies:
            copy.start()
        started.extend(copies)

    def receive(slot):
        for copy in block_copies(slot, 0, partners[0]):
            copy.wait_recv()

    places = groups * size_y * size_c

    def split(slot):
        whole = blocks[slot].astype(jnp.int32).astype(jnp.float32)
        upper = whole.astype(jnp.bfloat16)
        halves[slot] = upper
        halves[places + slot] = (whole - upper.astype(jnp.float32)).astype(jnp.bfloat16)

    def send_core(slot):
        for to in line_c:
            send(slot, (group, index(z, y, to)))

    for to_g, to_y in across:
        send(home, (to_g, index(z, to_y, core)))
    send_core(home)
    with jax.named_scope("spread_levels"):
        loads[6].wait()
        spreads[z] = (spread_own[...] * LEVELS + 0.5).astype(jnp.int32).astype(jnp.int16)
    table_copies = []
    for k, to in enumerate(send_z):
        for which, (source, landing) in enumerate(((travel_ref, travels), (spreads.at[z], spreads))):
            copy = pltpu.make_async_remote_copy(
                src_ref=source,
                dst_ref=landing.at[z],
                send_sem=table_send.at[which, k],
                recv_sem=table_recv.at[which, z],
                device_id=(group, index(to, y, core)),
                device_id_type=MESH,
            )
            copy.start()
            table_copies.append(copy)

    with jax.named_scope("picks"):
        lane = lax.broadcasted_iota(jnp.int32, (rows, 2 * half), 1)
        tiles = [index(to, y, core) for to in (*line_z, z)]
        pick_weight = jnp.concatenate([jnp.where(lane == tile, 1.0, 0.0) for tile in tiles], axis=0).astype(jnp.bfloat16)
        pick_row = jnp.concatenate([jnp.where(lane == tile + half, 1.0, 0.0) for tile in tiles], axis=0).astype(jnp.bfloat16)
    split(home)
    for at_g, at_y in across[::-1]:
        slot = slot_of(at_g, at_y, core)
        receive(slot)
        send_core(slot)
        split(slot)
    for at_c in line_c:
        receive(slot_of(group, y, at_c))
        split(slot_of(group, y, at_c))
    for at_g, at_y in across[::-1]:
        for at_c in line_c:
            receive(slot_of(at_g, at_y, at_c))
            split(slot_of(at_g, at_y, at_c))

    total = places * count
    with jax.named_scope("stack"):
        chosen = picks[...].reshape(total, 2 * half)
        dims = (((1,), (1,)), ((), ()))
        weight = lax.dot_general(pick_weight, chosen, dims, preferred_element_type=jnp.float32)
        row = lax.dot_general(pick_row, chosen, dims, preferred_element_type=jnp.float32)
        wanted = lax.rem(lax.broadcasted_iota(jnp.int32, row.shape, 0), rows).astype(jnp.float32)
        member = jnp.where(row == wanted, weight, 0.0).astype(jnp.bfloat16)
        member = jnp.concatenate([member, member], axis=1)
        data = halves[...].reshape(2 * total, samples)
        stacks = jnp.dot(member, data, preferred_element_type=jnp.float32)
        uppers = pltpu.roll(stacks, samples - 1, 1)

    part_copies = []
    with jax.named_scope("other_images"):
        for k, to in enumerate(line_z):
            mine = slice(k * rows, (k + 1) * rows)
            for which, landing in enumerate((travels, spreads)):
                pltpu.make_async_remote_copy(
                    src_ref=landing.at[to],
                    dst_ref=landing.at[to],
                    send_sem=table_send.at[which, k],
                    recv_sem=table_recv.at[which, to],
                    device_id=(group, index(to, y, core)),
                    device_id_type=MESH,
                ).wait_recv()
            other = spreads[to].astype(jnp.int32).astype(jnp.float32)
            outgoing[k] = partial_image(stacks[mine], uppers[mine], travels[to], other) * (1.0 / LEVELS)
            copy = pltpu.make_async_remote_copy(
                src_ref=outgoing.at[k],
                dst_ref=parts.at[z],
                send_sem=part_send.at[k],
                recv_sem=part_recv.at[z],
                device_id=(group, index(to, y, core)),
                device_id_type=MESH,
            )
            copy.start()
            part_copies.append(copy)
    with jax.named_scope("own_image"):
        loads[5].wait()
        mine = slice((size_z - 1) * rows, size_z * rows)
        image = partial_image(stacks[mine], uppers[mine], travels[z], spread_own[...])
    with jax.named_scope("last_waits"):
        for copy in started:
            copy.wait_send()
        for copy in table_copies:
            copy.wait_send()
        for k, to in enumerate(line_z):
            pltpu.make_async_remote_copy(
                src_ref=outgoing.at[k],
                dst_ref=parts.at[to],
                send_sem=part_send.at[k],
                recv_sem=part_recv.at[to],
                device_id=(group, index(to, y, core)),
                device_id_type=MESH,
            ).wait_recv()
            image = image + parts[to]
        for copy in part_copies:
            copy.wait_send()
    out_ref[...] = image * (scale / LEVELS)


def per_device(traces, aperture, bucket, table_node, entry_gain, travel, spread):
    tiles = lax.axis_size("image")
    groups = lax.axis_size("table")
    count, samples = traces.shape
    nodes, cells = travel.shape[1], travel.shape[2]
    half = -(-tiles // (LANES // 2)) * (LANES // 2)
    sizes = split_axis(tiles)
    size_z, size_y = sizes[:2]
    plane = size_y * sizes[2]
    scale = 1.0 / math.sqrt(count * groups * aperture.shape[1])
    vmem = pl.BlockSpec(memory_space=pltpu.VMEM)
    whole = pl.BlockSpec(memory_space=pl.ANY)
    return pl.pallas_call(
        functools.partial(kernel, sizes, groups, half, scale),
        out_shape=jax.ShapeDtypeStruct((1, cells), jnp.float32),
        in_specs=[whole] * 7,
        out_specs=vmem,
        scratch_shapes=[
            pltpu.VMEM(aperture.shape[::-1], jnp.int32),
            pltpu.VMEM((1, count), jnp.int32),
            pltpu.VMEM(table_node.shape[::-1], jnp.int32),
            pltpu.VMEM(entry_gain.shape[::-1], jnp.bfloat16),
            pltpu.VMEM(traces.shape, jnp.bfloat16),
            pltpu.VMEM((groups * plane, count, samples), jnp.int16),
            pltpu.VMEM((groups * plane, count, 2 * half), jnp.bfloat16),
            pltpu.VMEM((2 * groups * plane, count, samples), jnp.bfloat16),
            pltpu.VMEM((size_z, nodes, cells), jnp.float32),
            pltpu.VMEM((nodes, cells), jnp.float32),
            pltpu.VMEM((size_z, nodes, cells), jnp.int16),
            pltpu.VMEM((size_z, 1, cells), jnp.float32),
            pltpu.VMEM((max(size_z - 1, 1), 1, cells), jnp.float32),
            pltpu.SemaphoreType.DMA((7,)),
            pltpu.SemaphoreType.DMA((2, groups * plane)),
            pltpu.SemaphoreType.DMA((2, groups * plane)),
            pltpu.SemaphoreType.DMA((2, max(size_z - 1, 1))),
            pltpu.SemaphoreType.DMA((2, size_z)),
            pltpu.SemaphoreType.DMA((max(size_z - 1, 1),)),
            pltpu.SemaphoreType.DMA((size_z,)),
        ],
        compiler_params=pltpu.CompilerParams(
            collective_id=0, has_side_effects=True, vmem_limit_bytes=24 * 1024 * 1024
        ),
        cost_estimate=pl.CostEstimate(flops=10**8, bytes_accessed=10**6, transcendentals=0),
    )(*(pltpu.with_memory_space_constraint(operand, pltpu.HBM) for operand in (
        aperture.T, bucket.reshape(1, count), table_node.T, entry_gain.T, traces, travel[0], spread[0]
    )))


def solution(mesh):
    in_specs = (
        P(("table", "image"), None),
        P(("table", "image"), None),
        P(("table", "image")),
        P(("table", "image"), None),
        P(("table", "image"), None),
        P("image", None, "table"),
        P("image", None, "table"),
    )
    out_specs = P("image", "table")
    return jax.shard_map(
        per_device, mesh=mesh, in_specs=in_specs, out_specs=out_specs, check_vma=False
    )
```
